32 devices in a mesh: groups: 2 (over x), fsdp: 2 (over core), tensor: 8 (over z, y).
Axes of the slice: x: 2, y: 2, z: 4, core: 2. Of those that a mesh axis runs over, the one named last changes fastest.
Arguments:
- hidden: bfloat16 [4, 64, 5120], P(None, ('groups', 'fsdp')), parts along dimension 1, may hold values from -6 to 6
- lengths: int32 [64], P(('groups', 'fsdp')), parts along dimension 0, may hold values from 1 to 2048, as said below
- key_cache: bfloat16 [64, 2048, 1024], P(('groups', 'fsdp'), 'tensor'), parts along dimension 0, may hold values from -200 to 200
- value_cache: bfloat16 [64, 2048, 1024], P(('groups', 'fsdp'), 'tensor'), parts along dimension 0, may hold values from -6 to 6
- w_query: bfloat16 [5120, 8192], P(None, 'tensor'), may hold values from -0.078125 to 0.078125
- w_key: bfloat16 [5120, 1024], P(None, 'tensor'), may hold values from -0.078125 to 0.078125
- w_value: bfloat16 [5120, 1024], P(None, 'tensor'), may hold values from -0.078125 to 0.078125
- w_out: bfloat16 [8192, 5120], P('tensor'), may hold values from -0.75 to 0.75
- down_q: bfloat16 [10240, 64], P(('groups', 'fsdp', 'tensor')), parts along dimension 0, may hold values from -0.078125 to 0.078125
- up_q: bfloat16 [64, 128, 128], P(None, ('groups', 'tensor'), 'fsdp'), parts along dimension 1, may hold values from -0.375 to 0.375
- down_o: bfloat16 [64, 256, 64], P('tensor', ('groups', 'fsdp')), parts along dimension 1, may hold values from -0.375 to 0.375
- up_o: bfloat16 [64, 10240], P(None, ('groups', 'fsdp', 'tensor')), parts along dimension 1, may hold values from -0.75 to 0.75
- out_gain: bfloat16 [5120], P('tensor'), may hold values from 0.5 to 1.5
Outputs:
- normed: bfloat16 [4, 64, 5120], P(None, ('groups', 'fsdp'), 'tensor'), parts along dimension 1
The draws below stay inside these ranges and needn't reach their ends.
There are 2 independent parts, one for each index of `groups`. The reference program is written for one: setup_inputs(seed, part) draws one part's arguments, and reference() takes and returns one part's arrays. A program takes and returns all parts, laid end to end along the dimension named above; an argument that names none is the same for every part. Nothing has to cross between parts.
Inputs may be any that keep to these rules, and one draw needn't show every extreme that they name: A row attends to the first lengths slots of its cache; in each block of 16 rows of one device the first row's cache is full.
All inputs are finite; a program needn't handle non-finite values.
Results may differ from the reference program's by a relative error of at most 0.033.
Values may be sent and summed in bfloat16 or wider, within the bound.
A program may use at most 128 MiB of HBM per device.

```python
import math
import jax
import jax.numpy as jnp
from jax import lax

D = 5120
HEADS = 64
KVH = 8
HD = 128
R = 64
ROWS_DEV = 16
CACHE = 2048
STEPS = 4
ROWS = 32


def draw_lengths(key, part):
    key = jax.random.fold_in(key, 11)
    drawn = jax.random.randint(key, (ROWS,), 1, CACHE + 1)
    row_index = jnp.arange(ROWS)
    return jnp.where(row_index % ROWS_DEV == 0, CACHE, drawn).astype(jnp.int32)


def draw_key_cache(key, part):
    key = jax.random.fold_in(key, 23)
    base_draw = jax.random.normal(key, (ROWS, CACHE, KVH * HD), jnp.float32)
    return jnp.clip(base_draw, -6.0, 6.0).astype(jnp.bfloat16)


def block_scale(rng, dims, cuts, low, largest):
    def one(axis_at, blocks):
        steps = jax.random.uniform(jax.random.fold_in(jax.random.fold_in(rng, 6), axis_at), (blocks,), jnp.float32, low / len(cuts), largest / len(cuts))
        return jnp.repeat(jnp.exp(steps), dims[axis_at] // blocks).reshape((-1,) + (1,) * (len(dims) - axis_at - 1))

    factor_of = one(*cuts[0])
    for cut in cuts[1:]:
        factor_of = factor_of * one(*cut)
    return factor_of


def gaussian(own_key, extent, spread, reach, shards=(), held_as=jnp.bfloat16):
    level = block_scale(own_key, extent, shards, -0.22, 0.18) if shards else 1.0
    array = jax.random.normal(own_key, extent, jnp.float32) * spread * level
    return jnp.minimum(jnp.maximum(array, -reach), reach).astype(held_as)


def setup_inputs(seed: int = 0, part: int = 0) -> dict:
    key_of = jax.random.split(jax.random.key(seed), 14)
    part_keys = jax.random.split(jax.random.fold_in(key_of[13], part), 14)
    hidden = gaussian(part_keys[0], (STEPS, ROWS, D), 1.0, 6.0, ((1, 2),))
    lengths = draw_lengths(jax.random.fold_in(jax.random.fold_in(key_of[13], part), 71), part)
    key_cache = draw_key_cache(jax.random.fold_in(jax.random.fold_in(key_of[13], part), 71), part)
    value_cache = gaussian(part_keys[3], (ROWS, CACHE, KVH * HD), 1.0, 6.0, ((0, 2), (1, 8)))
    w_query = gaussian(key_of[4], (D, HEADS * HD), D ** -0.5, 0.078125, ((1, 8),))
    w_key = gaussian(key_of[5], (D, KVH * HD), D ** -0.5, 0.078125, ((1, 8),))
    w_value = gaussian(key_of[6], (D, KVH * HD), D ** -0.5, 0.078125, ((1, 8),))
    w_out = gaussian(key_of[7], (HEADS * HD, D), (HD // 2) ** -0.5, 0.75, ((0, 8),))
    down_q = gaussian(part_keys[8], (D, R), D ** -0.5, 0.078125, ((0, 16),))
    up_q = gaussian(part_keys[9], (R, HEADS, HD), (4 * R) ** -0.5, 0.375, ((1, 8), (2, 2)))
    down_o = gaussian(part_keys[10], (HEADS, HD, R), (4 * R) ** -0.5, 0.375, ((0, 8), (1, 2)))
    up_o = gaussian(part_keys[11], (R, D), (HD // 2) ** -0.5, 0.75, ((1, 16),))
    out_gain = jnp.clip(1.0 + 0.1 * jax.random.normal(key_of[12], (D,), jnp.float32), 0.5, 1.5).astype(jnp.bfloat16)
    return dict(hidden=hidden, lengths=lengths, key_cache=key_cache, value_cache=value_cache, w_query=w_query, w_key=w_key, w_value=w_value, w_out=w_out, down_q=down_q, up_q=up_q, down_o=down_o, up_o=up_o, out_gain=out_gain)


rope_base = 1000000.0
norm_eps = 1e-06

def rotate(values_in, position):
    half_dim = values_in.shape[-1] // 2
    exponent = jnp.arange(half_dim, dtype=jnp.float32) * (2.0 / values_in.shape[-1])
    frequency = jnp.exp(-exponent * math.log(rope_base))
    angles = position[..., None] * frequency
    cosine = jnp.cos(angles)
    sine = jnp.sin(angles)
    first_half = values_in[..., :half_dim]
    second_half = values_in[..., half_dim:]
    return jnp.concatenate([first_half * cosine - second_half * sine, second_half * cosine + first_half * sine], -1)

def reference(hidden, lengths, key_cache, value_cache, w_query, w_key, w_value, w_out, down_q, up_q, down_o, up_o, out_gain):
    group_size = HEADS // KVH
    score_scale = HD ** (-0.5)
    merged_query = (w_query.astype(jnp.float32) + jnp.dot(down_q, up_q.reshape(R, HEADS * HD), preferred_element_type=jnp.float32)).astype(jnp.bfloat16)
    merged_out = (w_out.astype(jnp.float32) + jnp.dot(down_o.reshape(HEADS * HD, R), up_o, preferred_element_type=jnp.float32)).astype(jnp.bfloat16)
    new_keys = []
    new_values = []
    results = []
    for step_index in range(STEPS):
        step_input = hidden[step_index]
        position = (lengths + step_index).astype(jnp.float32)
        query = rotate(jnp.dot(step_input, merged_query, preferred_element_type=jnp.float32).reshape(ROWS, HEADS, HD), position[:, None]).astype(jnp.bfloat16)
        key_raw = jnp.dot(step_input, w_key, preferred_element_type=jnp.float32).astype(jnp.bfloat16)
        key_raw = lax.optimization_barrier(key_raw)
        key_new = rotate(key_raw.astype(jnp.float32).reshape(ROWS, KVH, HD), position[:, None]).astype(jnp.bfloat16)
        value_new = jnp.dot(step_input, w_value, preferred_element_type=jnp.float32).astype(jnp.bfloat16).reshape(ROWS, KVH, HD)
        new_keys.append(key_new)
        new_values.append(value_new)
        fresh_keys = jnp.stack(new_keys, 1)
        fresh_values = jnp.stack(new_values, 1)
        fresh_count = step_index + 1

        def one_row(items):
            row_query, row_keys, row_values, row_fresh_k, row_fresh_v, row_length = items
            all_keys = jnp.concatenate([row_keys.reshape(CACHE, KVH, HD), row_fresh_k], 0).astype(jnp.float32)
            all_values = jnp.concatenate([row_values.reshape(CACHE, KVH, HD), row_fresh_v], 0).astype(jnp.float32)
            grouped = row_query.reshape(KVH, group_size, HD).astype(jnp.float32)
            scores = jnp.einsum('kgd,pkd->kgp', grouped, all_keys) * score_scale
            live_mask = jnp.concatenate([jnp.arange(CACHE, dtype=jnp.int32) < row_length, jnp.ones((fresh_count,), dtype=bool)])
            peak_score = lax.optimization_barrier(jnp.max(jnp.where(live_mask, scores, jnp.float32(-1e+30)), -1))
            weights = jnp.where(live_mask, jnp.exp(scores - peak_score[..., None]), jnp.float32(0.0))
            weight_sum = lax.optimization_barrier(jnp.sum(weights, -1))
            rounded = weights.astype(jnp.bfloat16).astype(jnp.float32)
            mixed_sum = jnp.einsum('kgp,pkd->kgd', rounded, all_values)
            return (mixed_sum / weight_sum[..., None]).reshape(HEADS * HD)
        attended = lax.map(one_row, (query, key_cache, value_cache, fresh_keys, fresh_values, lengths)).astype(jnp.bfloat16)
        stream = step_input.astype(jnp.float32) + jnp.dot(attended, merged_out, preferred_element_type=jnp.float32)
        factor = lax.rsqrt(lax.optimization_barrier(jnp.mean(stream * stream, -1, keepdims=True)) + norm_eps)
        results.append((stream * factor * out_gain.astype(jnp.float32)).astype(jnp.bfloat16))
    return jnp.stack(results)
```

```python
import math

import jax
import jax.numpy as jnp
from jax import lax
from jax.sharding import PartitionSpec as P

HEADS = 64
KVH = 8
HD = 128
R = 64
STEPS = 4
GROUP = HEADS // KVH

rope_base = 1000000.0
norm_eps = 1e-06
F32 = jnp.float32
BF16 = jnp.bfloat16


def rotate(values_in, position):
    half_dim = values_in.shape[-1] // 2
    exponent = jnp.arange(half_dim, dtype=F32) * (2.0 / values_in.shape[-1])
    frequency = jnp.exp(-exponent * math.log(rope_base))
    angles = position[..., None] * frequency
    cosine = jnp.cos(angles)
    sine = jnp.sin(angles)
    first_half = values_in[..., :half_dim]
    second_half = values_in[..., half_dim:]
    return jnp.concatenate(
        [first_half * cosine - second_half * sine, second_half * cosine + first_half * sine], -1
    )


def dot(a, b):
    return jnp.dot(a, b, preferred_element_type=F32)


def shards(
    hidden, lengths, key_cache, value_cache, w_query, w_key, w_value, w_out,
    down_q, up_q, down_o, up_o, out_gain,
):
    tc = lax.axis_size("tensor")
    ti = lax.axis_index("tensor")
    rows = hidden.shape[1]
    width = hidden.shape[2]
    hh = w_query.shape[1] // HD
    scale = HD ** (-0.5)
    share = width // tc
    cache = key_cache.shape[1]
    n = STEPS * rows
    x = hidden.reshape(n, width)
    up_flat = lax.all_gather(up_q, "fsdp", axis=2, tiled=True).reshape(R, hh * HD)
    down_flat = lax.all_gather(down_o, "fsdp", axis=1, tiled=True).reshape(hh * HD, R)
    down_all = lax.all_gather(down_q, ("fsdp", "tensor"), axis=0, tiled=True)
    up_all = lax.all_gather(up_o, ("fsdp", "tensor"), axis=1, tiled=True)
    position = (lengths[None, :] + jnp.arange(STEPS, dtype=jnp.int32)[:, None]).astype(F32)
    query = dot(x, w_query) + dot(dot(x, down_all).astype(BF16), up_flat)
    query = rotate(query.reshape(STEPS, rows, hh, HD), position[:, :, None]).astype(BF16)
    key_raw = dot(x, w_key).astype(BF16)
    value_new = dot(x, w_value).astype(BF16)
    if hh != GROUP:
        key_raw = lax.all_gather(key_raw, "tensor", axis=1, tiled=True)
        value_new = lax.all_gather(value_new, "tensor", axis=1, tiled=True)
        kv_at = (ti * hh) // GROUP * HD
        key_raw = lax.dynamic_slice_in_dim(key_raw, kv_at, HD, 1)
        value_new = lax.dynamic_slice_in_dim(value_new, kv_at, HD, 1)
    key_raw = key_raw.astype(F32).reshape(STEPS, rows, HD)
    key_new = rotate(key_raw, position).astype(BF16)
    value_new = value_new.reshape(STEPS, rows, HD)

    query_all = lax.all_gather(query, "tensor", axis=2, tiled=True)
    grouped = query_all.reshape(STEPS, rows, KVH, GROUP, HD).transpose(1, 2, 0, 3, 4)
    grouped = grouped.reshape(rows, KVH, STEPS * GROUP, HD)
    keys = key_cache.reshape(rows, cache, KVH, HD)
    values = value_cache.reshape(rows, cache, KVH, HD)
    scores = jnp.einsum("rkgd,rpkd->rkgp", grouped, keys, preferred_element_type=F32) * scale
    slot = ti * cache + jnp.arange(cache, dtype=jnp.int32)
    live = (slot[None, :] < lengths[:, None])[:, None, None, :]
    peak = jnp.max(jnp.where(live, scores, F32(-1e30)), -1)
    weights = jnp.where(live, jnp.exp(scores - peak[..., None]), F32(0.0))
    wsum = jnp.sum(weights, -1)
    mixed = jnp.einsum(
        "rkgp,rpkd->rkgd", weights.astype(BF16), values, preferred_element_type=F32
    )
    mixed = mixed.reshape(rows, KVH, STEPS, GROUP, HD).transpose(0, 1, 3, 2, 4)
    mixed = mixed.reshape(rows, HEADS, STEPS, HD)
    stats = jnp.stack([peak, wsum], 0).reshape(2, rows, KVH, STEPS, GROUP)
    stats = stats.transpose(0, 1, 2, 4, 3).reshape(2, rows, HEADS, STEPS)
    got_mixed = lax.all_to_all(
        mixed.astype(BF16), "tensor", split_axis=1, concat_axis=1, tiled=True
    ).astype(F32)
    got_stats = lax.all_to_all(stats, "tensor", split_axis=2, concat_axis=2, tiled=True)
    got_mixed = got_mixed.reshape(rows, tc, hh, STEPS, HD).swapaxes(2, 3)
    got_peak = got_stats[0].reshape(rows, tc, hh, STEPS).swapaxes(2, 3)
    got_sum = got_stats[1].reshape(rows, tc, hh, STEPS).swapaxes(2, 3)

    own = (
        jnp.einsum("srhd,trd->rsht", query, key_new, preferred_element_type=F32) * scale
    )
    causal = jnp.tril(jnp.ones((STEPS, STEPS), bool))[None, :, None, :]
    own_peak = jnp.max(jnp.where(causal, own, F32(-1e30)), -1)
    top = jnp.maximum(jnp.max(got_peak, 1), own_peak)
    own_w = jnp.where(causal, jnp.exp(own - top[..., None]), F32(0.0))
    far = jnp.exp(got_peak - top[:, None])
    den = jnp.sum(far * got_sum, 1) + jnp.sum(own_w, -1)
    num = jnp.sum(far[..., None] * got_mixed, 1) + jnp.einsum(
        "rsht,trd->rshd", own_w.astype(BF16), value_new, preferred_element_type=F32
    )
    attended = (num / den[..., None]).astype(BF16).transpose(1, 0, 2, 3).reshape(n, hh * HD)
    part = dot(attended, w_out) + dot(dot(attended, down_flat).astype(BF16), up_all)
    own_cols = lax.psum_scatter(part, "tensor", scatter_dimension=1, tiled=True)
    own_cols = own_cols + lax.dynamic_slice_in_dim(x, ti * share, share, 1).astype(F32)
    square = lax.psum(jnp.sum(own_cols * own_cols, -1, keepdims=True), "tensor")
    factor = lax.rsqrt(square / width + norm_eps)
    return (own_cols * factor * out_gain.astype(F32)).astype(BF16).reshape(STEPS, rows, share)


def solution(mesh):
    both = ("groups", "fsdp")
    placed = (
        P(None, both, None),
        P(both),
        P(both, "tensor", None),
        P(both, "tensor", None),
        P(None, "tensor"),
        P(None, "tensor"),
        P(None, "tensor"),
        P("tensor", None),
        P(("groups", "fsdp", "tensor"), None),
        P(None, ("groups", "tensor"), "fsdp"),
        P("tensor", both, None),
        P(None, ("groups", "fsdp", "tensor")),
        P("tensor"),
    )
    return jax.shard_map(
        shards,
        mesh=mesh,
        in_specs=placed,
        out_specs=P(None, both, "tensor"),
        check_vma=False,
    )
```

```python
import math

import jax
import jax.numpy as jnp
from jax import lax
from jax.sharding import PartitionSpec as P

HEADS = 64
KVH = 8
HD = 128
R = 64
STEPS = 4
GROUP = HEADS // KVH

rope_base = 1000000.0
norm_eps = 1e-06
F32 = jnp.float32
BF16 = jnp.bfloat16


def rotate(values_in, position):
    half_dim = values_in.shape[-1] // 2
    exponent = jnp.arange(half_dim, dtype=F32) * (2.0 / values_in.shape[-1])
    frequency = jnp.exp(-exponent * math.log(rope_base))
    angles = position[..., None] * frequency
    cosine = jnp.cos(angles)
    sine = jnp.sin(angles)
    first_half = values_in[..., :half_dim]
    second_half = values_in[..., half_dim:]
    return jnp.concatenate(
        [first_half * cosine - second_half * sine, second_half * cosine + first_half * sine], -1
    )


def dot(a, b):
    return jnp.dot(a, b, preferred_element_type=F32)


def spread(value):
    count = lax.axis_size("tensor")
    return lax.all_to_all(jnp.broadcast_to(value[None], (count,) + value.shape), "tensor", 0, 0)


def pair(value, axis):
    if lax.axis_size("fsdp") != 2:
        return lax.all_gather(value, "fsdp", axis=axis, tiled=True)
    other = lax.ppermute(value, "fsdp", [(0, 1), (1, 0)])
    first = lax.axis_index("fsdp") == 0
    return jnp.concatenate(
        [jnp.where(first, value, other), jnp.where(first, other, value)], axis
    )


def attend(grouped, key_cache, value_cache, live_count):
    rows, cache = key_cache.shape[:2]
    keys = key_cache.reshape(rows, cache, KVH, HD)
    values = value_cache.reshape(rows, cache, KVH, HD)
    scores = jnp.einsum("krmd,rpkd->krmp", grouped, keys, preferred_element_type=F32)
    scores = scores * HD ** (-0.5)
    slot = jnp.arange(cache, dtype=jnp.int32)
    live = (slot[None, :] < live_count[:, None])[None, :, None, :]
    peak = jnp.max(jnp.where(live, scores, F32(-1e30)), -1)
    weights = jnp.where(live, jnp.exp(scores - peak[..., None]), F32(0.0))
    mixed = jnp.einsum("krmp,rpkd->krmd", weights.astype(BF16), values, preferred_element_type=F32)
    return mixed.astype(BF16), peak, jnp.sum(weights, -1)


def shards(
    hidden, lengths, key_cache, value_cache, w_query, w_key, w_value, w_out,
    down_q, up_q, down_o, up_o, out_gain,
):
    tc = lax.axis_size("tensor")
    ti = lax.axis_index("tensor")
    rows = hidden.shape[1]
    width = hidden.shape[2]
    hh = w_query.shape[1] // HD
    scale = HD ** (-0.5)
    share = width // tc
    cache = key_cache.shape[1]
    n = STEPS * rows
    x = hidden.reshape(n, width)
    up_flat = pair(up_q, 2).reshape(R, hh * HD)
    down_flat = pair(down_o, 1).reshape(hh * HD, R)
    nf = lax.axis_size("fsdp")
    chunk = down_q.shape[0]
    spots = [(c, (c % nf) * tc + c // nf) for c in range(nf * tc)]
    up_cols = pair(lax.ppermute(up_o, ("fsdp", "tensor"), spots), 1)
    down_pair = pair(down_q, 0)
    x_pair = jnp.concatenate(
        [
            lax.dynamic_slice_in_dim(x, (f * tc + ti) * chunk, chunk, 1)
            for f in range(nf)
        ],
        1,
    )
    thin = jnp.sum(spread(dot(x_pair, down_pair)), 0)
    position = (lengths[None, :] + jnp.arange(STEPS, dtype=jnp.int32)[:, None]).astype(F32)
    query = dot(x, w_query) + dot(thin.astype(BF16), up_flat)
    query = rotate(query.reshape(STEPS, rows, hh, HD), position[:, :, None]).astype(BF16)
    key_raw = dot(x, w_key).astype(BF16)
    value_new = dot(x, w_value).astype(BF16)
    if hh != GROUP:
        key_raw = lax.all_gather(key_raw, "tensor", axis=1, tiled=True)
        value_new = lax.all_gather(value_new, "tensor", axis=1, tiled=True)
        kv_at = (ti * hh) // GROUP * HD
        key_raw = lax.dynamic_slice_in_dim(key_raw, kv_at, HD, 1)
        value_new = lax.dynamic_slice_in_dim(value_new, kv_at, HD, 1)
    key_raw = key_raw.astype(F32).reshape(STEPS, rows, HD)
    key_new = rotate(key_raw, position).astype(BF16)
    value_new = value_new.reshape(STEPS, rows, HD)

    query_all = spread(query)
    per = tc // KVH
    grouped = query_all.reshape(KVH, per, STEPS, rows, hh, HD).transpose(0, 3, 2, 1, 4, 5)
    grouped = grouped.reshape(KVH, rows, STEPS * GROUP, HD)
    mixed, peak, wsum = attend(grouped, key_cache, value_cache, lengths - ti * cache)
    mixed = mixed.reshape(KVH, rows, STEPS, per, hh, HD).transpose(0, 3, 1, 2, 4, 5)
    mixed = mixed.reshape(tc, rows, STEPS, hh, HD)
    stats = jnp.stack([peak, wsum], 2).reshape(KVH, rows, 2, STEPS, per, hh)
    stats = stats.transpose(0, 4, 1, 2, 3, 5).reshape(tc, rows, 2, STEPS, hh)
    got_mixed = lax.all_to_all(mixed, "tensor", 0, 0).astype(F32)
    got_stats = lax.all_to_all(stats, "tensor", 0, 0)
    got_peak = got_stats[:, :, 0]
    got_sum = got_stats[:, :, 1]

    own = (
        jnp.einsum("srhd,trd->rsht", query, key_new, preferred_element_type=F32) * scale
    )
    causal = jnp.tril(jnp.ones((STEPS, STEPS), bool))[None, :, None, :]
    own_peak = jnp.max(jnp.where(causal, own, F32(-1e30)), -1)
    top = jnp.maximum(jnp.max(got_peak, 0), own_peak)
    own_w = jnp.where(causal, jnp.exp(own - top[..., None]), F32(0.0))
    far = jnp.exp(got_peak - top[None])
    den = jnp.sum(far * got_sum, 0) + jnp.sum(own_w, -1)
    num = jnp.sum(far[..., None] * got_mixed, 0) + jnp.einsum(
        "rsht,trd->rshd", own_w.astype(BF16), value_new, preferred_element_type=F32
    )
    attended = (num / den[..., None]).astype(BF16).transpose(1, 0, 2, 3).reshape(n, hh * HD)
    part = dot(attended, w_out).astype(BF16).reshape(n, tc, share).transpose(1, 0, 2)
    thin_out = dot(attended, down_flat)
    high = thin_out.astype(BF16)
    low = (thin_out - high.astype(F32)).astype(BF16)
    both = jnp.broadcast_to(jnp.concatenate([high, low], 1)[None], (tc, n, 2 * R))
    sent = jnp.concatenate([part, both], 2)
    total = jnp.sum(lax.all_to_all(sent, "tensor", 0, 0).astype(F32), 0)
    thin_out = (total[:, share : share + R] + total[:, share + R :]).astype(BF16)
    own_cols = total[:, :share] + dot(thin_out, up_cols)
    own_cols = own_cols + lax.dynamic_slice_in_dim(x, ti * share, share, 1).astype(F32)
    square = jnp.sum(spread(jnp.sum(own_cols * own_cols, -1)), 0)
    factor = lax.rsqrt(square / width + norm_eps)[:, None]
    return (own_cols * factor * out_gain.astype(F32)).astype(BF16).reshape(STEPS, rows, share)


def solution(mesh):
    both = ("groups", "fsdp")
    placed = (
        P(None, both, None),
        P(both),
        P(both, "tensor", None),
        P(both, "tensor", None),
        P(None, "tensor"),
        P(None, "tensor"),
        P(None, "tensor"),
        P("tensor", None),
        P(("groups", "fsdp", "tensor"), None),
        P(None, ("groups", "tensor"), "fsdp"),
        P("tensor", both, None),
        P(None, ("groups", "fsdp", "tensor")),
        P("tensor"),
    )
    return jax.shard_map(
        shards,
        mesh=mesh,
        in_specs=placed,
        out_specs=P(None, both, "tensor"),
        check_vma=False,
    )
```

```python
import functools
import math

import jax
import jax.numpy as jnp
from jax import lax
from jax.experimental import pallas as pl
from jax.experimental.pallas import tpu as pltpu
from jax.sharding import PartitionSpec as P

HEADS = 64
KVH = 8
HD = 128
R = 64
STEPS = 4
GROUP = HEADS // KVH

rope_base = 1000000.0
norm_eps = 1e-06
F32 = jnp.float32
BF16 = jnp.bfloat16


def rotate(values_in, position):
    half_dim = values_in.shape[-1] // 2
    exponent = jnp.arange(half_dim, dtype=F32) * (2.0 / values_in.shape[-1])
    frequency = jnp.exp(-exponent * math.log(rope_base))
    angles = position[..., None] * frequency
    cosine = jnp.cos(angles)
    sine = jnp.sin(angles)
    first_half = values_in[..., :half_dim]
    second_half = values_in[..., half_dim:]
    return jnp.concatenate(
        [first_half * cosine - second_half * sine, second_half * cosine + first_half * sine], -1
    )


def dot(a, b):
    return jnp.dot(a, b, preferred_element_type=F32)


def exchange_kernel(count, each, *refs):
    k = len(each)
    ins, outs = refs[:k], refs[k : 2 * k]
    send_sem, recv_sem, local_sem = refs[2 * k :]
    me = lax.axis_index("tensor")
    barrier = pltpu.get_barrier_semaphore()
    peers = [lax.rem(me + offset, count) for offset in range(1, count)]
    for peer in peers:
        pl.semaphore_signal(
            barrier, inc=1, device_id={"tensor": peer}, device_id_type=pl.DeviceIdType.MESH
        )
    locals_here = []
    for i in range(k):
        source = ins[i].at[me] if each[i] else ins[i]
        locals_here.append(pltpu.make_async_copy(source, outs[i].at[me], local_sem.at[i]))
        locals_here[-1].start()
    pl.semaphore_wait(barrier, count - 1)
    copies = []
    for at, peer in enumerate(peers):
        for i in range(k):
            copy = pltpu.make_async_remote_copy(
                src_ref=ins[i].at[peer] if each[i] else ins[i],
                dst_ref=outs[i].at[me],
                send_sem=send_sem.at[i, at],
                recv_sem=recv_sem.at[i, at],
                device_id={"tensor": peer},
                device_id_type=pl.DeviceIdType.MESH,
            )
            copy.start()
            copies.append(copy)
    for copy in locals_here + copies:
        copy.wait()


def exchange(ident, each, *arrays):
    count = lax.axis_size("tensor")
    if count != KVH:
        return [
            lax.all_to_all(
                a if e else jnp.broadcast_to(a[None], (count,) + a.shape), "tensor", 0, 0
            )
            for e, a in zip(each, arrays)
        ]
    k = len(arrays)
    shapes = [a.shape if e else (count,) + a.shape for e, a in zip(each, arrays)]
    vmem = pl.BlockSpec(memory_space=pltpu.VMEM)
    return pl.pallas_call(
        functools.partial(exchange_kernel, count, each),
        out_shape=[jax.ShapeDtypeStruct(d, a.dtype) for d, a in zip(shapes, arrays)],
        in_specs=[vmem] * k,
        out_specs=[vmem] * k,
        scratch_shapes=[
            pltpu.SemaphoreType.DMA((k, count - 1)),
            pltpu.SemaphoreType.DMA((k, count - 1)),
            pltpu.SemaphoreType.DMA((k,)),
        ],
        compiler_params=pltpu.CompilerParams(
            collective_id=ident, has_side_effects=True, vmem_limit_bytes=16 * 2**20
        ),
    )(*arrays)


def pair(value, axis):
    if lax.axis_size("fsdp") != 2:
        return lax.all_gather(value, "fsdp", axis=axis, tiled=True)
    other = lax.ppermute(value, "fsdp", [(0, 1), (1, 0)])
    first = lax.axis_index("fsdp") == 0
    return jnp.concatenate(
        [jnp.where(first, value, other), jnp.where(first, other, value)], axis
    )


def attend(grouped, key_cache, value_cache, live_count):
    rows, cache = key_cache.shape[:2]
    keys = key_cache.reshape(rows, cache, KVH, HD)
    values = value_cache.reshape(rows, cache, KVH, HD)
    scores = jnp.einsum("krmd,rpkd->krmp", grouped, keys, preferred_element_type=F32)
    scores = scores * HD ** (-0.5)
    slot = jnp.arange(cache, dtype=jnp.int32)
    live = (slot[None, :] < live_count[:, None])[None, :, None, :]
    peak = jnp.max(jnp.where(live, scores, F32(-1e30)), -1)
    weights = jnp.where(live, jnp.exp(scores - peak[..., None]), F32(0.0))
    mixed = jnp.einsum("krmp,rpkd->krmd", weights.astype(BF16), values, preferred_element_type=F32)
    return mixed.astype(BF16), peak, jnp.sum(weights, -1)


def shards(
    hidden, lengths, key_cache, value_cache, w_query, w_key, w_value, w_out,
    down_q, up_q, down_o, up_o, out_gain,
):
    tc = lax.axis_size("tensor")
    ti = lax.axis_index("tensor")
    rows = hidden.shape[1]
    width = hidden.shape[2]
    hh = w_query.shape[1] // HD
    scale = HD ** (-0.5)
    share = width // tc
    cache = key_cache.shape[1]
    n = STEPS * rows
    x = hidden.reshape(n, width)
    up_flat = pair(up_q, 2).reshape(R, hh * HD)
    down_flat = pair(down_o, 1).reshape(hh * HD, R)
    nf = lax.axis_size("fsdp")
    chunk = down_q.shape[0]
    spots = [(c, (c % nf) * tc + c // nf) for c in range(nf * tc)]
    up_cols = pair(lax.ppermute(up_o, ("fsdp", "tensor"), spots), 1)
    down_pair = pair(down_q, 0)
    x_pair = jnp.concatenate(
        [
            lax.dynamic_slice_in_dim(x, (f * tc + ti) * chunk, chunk, 1)
            for f in range(nf)
        ],
        1,
    )
    thin = dot(x_pair, down_pair)
    thin = jnp.concatenate([thin, jnp.zeros_like(thin)], 1)
    thin = jnp.sum(exchange(0, (False,), thin)[0], 0)[:, :R]
    position = (lengths[None, :] + jnp.arange(STEPS, dtype=jnp.int32)[:, None]).astype(F32)
    query = dot(x, w_query) + dot(thin.astype(BF16), up_flat)
    query = rotate(query.reshape(STEPS, rows, hh, HD), position[:, :, None]).astype(BF16)
    key_raw = dot(x, w_key).astype(BF16)
    value_new = dot(x, w_value).astype(BF16)
    if hh != GROUP:
        key_raw = lax.all_gather(key_raw, "tensor", axis=1, tiled=True)
        value_new = lax.all_gather(value_new, "tensor", axis=1, tiled=True)
        kv_at = (ti * hh) // GROUP * HD
        key_raw = lax.dynamic_slice_in_dim(key_raw, kv_at, HD, 1)
        value_new = lax.dynamic_slice_in_dim(value_new, kv_at, HD, 1)
    key_raw = key_raw.astype(F32).reshape(STEPS, rows, HD)
    key_new = rotate(key_raw, position).astype(BF16)
    value_new = value_new.reshape(STEPS, rows, HD)

    query, up_cols, down_flat = lax.optimization_barrier((query, up_cols, down_flat))
    query_all = exchange(1, (False,), query.reshape(n, hh * HD))[0]
    per = tc // KVH
    grouped = query_all.reshape(KVH, per, STEPS, rows, hh, HD).transpose(0, 3, 2, 1, 4, 5)
    grouped = grouped.reshape(KVH, rows, STEPS * GROUP, HD)
    mixed, peak, wsum = attend(grouped, key_cache, value_cache, lengths - ti * cache)
    mixed = mixed.reshape(KVH, rows, STEPS, per, hh, HD).transpose(0, 3, 1, 2, 4, 5)
    mixed = mixed.reshape(tc, n * hh, HD)
    stats = jnp.stack([peak, wsum], 2).reshape(KVH, rows, 2, STEPS, per, hh)
    stats = stats.transpose(0, 4, 1, 2, 3, 5).reshape(tc, n * hh // 64, 128)
    got_mixed, got_stats = exchange(2, (True, True), mixed, stats)
    got_mixed = got_mixed.astype(F32).reshape(tc, rows, STEPS, hh, HD)
    got_stats = got_stats.reshape(tc, rows, 2, STEPS, hh)
    got_peak = got_stats[:, :, 0]
    got_sum = got_stats[:, :, 1]

    own = (
        jnp.einsum("srhd,trd->rsht", query, key_new, preferred_element_type=F32) * scale
    )
    causal = jnp.tril(jnp.ones((STEPS, STEPS), bool))[None, :, None, :]
    own_peak = jnp.max(jnp.where(causal, own, F32(-1e30)), -1)
    top = jnp.maximum(jnp.max(got_peak, 0), own_peak)
    own_w = jnp.where(causal, jnp.exp(own - top[..., None]), F32(0.0))
    far = jnp.exp(got_peak - top[None])
    den = jnp.sum(far * got_sum, 0) + jnp.sum(own_w, -1)
    num = jnp.sum(far[..., None] * got_mixed, 0) + jnp.einsum(
        "rsht,trd->rshd", own_w.astype(BF16), value_new, preferred_element_type=F32
    )
    attended = (num / den[..., None]).astype(BF16).transpose(1, 0, 2, 3).reshape(n, hh * HD)
    part = dot(attended, w_out).astype(BF16).reshape(n, tc, share).transpose(1, 0, 2)
    thin_out = dot(attended, down_flat)
    high = thin_out.astype(BF16)
    low = (thin_out - high.astype(F32)).astype(BF16)
    both = jnp.broadcast_to(jnp.concatenate([high, low], 1)[None], (tc, n, 2 * R))
    sent = jnp.concatenate([part, both], 2)
    total = jnp.sum(exchange(3, (True,), sent)[0].astype(F32), 0)
    thin_out = (total[:, share : share + R] + total[:, share + R :]).astype(BF16)
    own_cols = total[:, :share] + dot(thin_out, up_cols)
    own_cols = own_cols + lax.dynamic_slice_in_dim(x, ti * share, share, 1).astype(F32)
    square = jnp.sum(own_cols * own_cols, -1, keepdims=True)
    square = jnp.sum(exchange(4, (False,), jnp.broadcast_to(square, (n, 128)))[0], 0)
    factor = lax.rsqrt(square[:, :1] / width + norm_eps)
    return (own_cols * factor * out_gain.astype(F32)).astype(BF16).reshape(STEPS, rows, share)


def solution(mesh):
    both = ("groups", "fsdp")
    placed = (
        P(None, both, None),
        P(both),
        P(both, "tensor", None),
        P(both, "tensor", None),
        P(None, "tensor"),
        P(None, "tensor"),
        P(None, "tensor"),
        P("tensor", None),
        P(("groups", "fsdp", "tensor"), None),
        P(None, ("groups", "tensor"), "fsdp"),
        P("tensor", both, None),
        P(None, ("groups", "fsdp", "tensor")),
        P("tensor"),
    )
    return jax.shard_map(
        shards,
        mesh=mesh,
        in_specs=placed,
        out_specs=P(None, both, "tensor"),
        check_vma=False,
    )
```

```python
import functools
import math

import jax
import jax.numpy as jnp
from jax import lax
from jax.experimental import pallas as pl
from jax.experimental.pallas import tpu as pltpu
from jax.sharding import PartitionSpec as P

HEADS = 64
KVH = 8
HD = 128
R = 64
STEPS = 4
GROUP = HEADS // KVH

rope_base = 1000000.0
norm_eps = 1e-06
F32 = jnp.float32
BF16 = jnp.bfloat16


def rotate(values_in, position):
    half_dim = values_in.shape[-1] // 2
    exponent = jnp.arange(half_dim, dtype=F32) * (2.0 / values_in.shape[-1])
    frequency = jnp.exp(-exponent * math.log(rope_base))
    angles = position[..., None] * frequency
    cosine = jnp.cos(angles)
    sine = jnp.sin(angles)
    first_half = values_in[..., :half_dim]
    second_half = values_in[..., half_dim:]
    return jnp.concatenate(
        [first_half * cosine - second_half * sine, second_half * cosine + first_half * sine], -1
    )


def dot(a, b):
    return jnp.dot(a, b, preferred_element_type=F32)


def exchange_kernel(count, each, *refs):
    k = len(each)
    ins, outs = refs[:k], refs[k : 2 * k]
    send_sem, recv_sem, local_sem = refs[2 * k :]
    me = lax.axis_index("tensor")
    barrier = pltpu.get_barrier_semaphore()
    peers = [lax.rem(me + offset, count) for offset in range(1, count)]
    for peer in peers:
        pl.semaphore_signal(
            barrier, inc=1, device_id={"tensor": peer}, device_id_type=pl.DeviceIdType.MESH
        )
    locals_here = []
    for i in range(k):
        source = ins[i].at[me] if each[i] else ins[i]
        locals_here.append(pltpu.make_async_copy(source, outs[i].at[me], local_sem.at[i]))
        locals_here[-1].start()
    pl.semaphore_wait(barrier, count - 1)
    copies = []
    for at, peer in enumerate(peers):
        for i in range(k):
            copy = pltpu.make_async_remote_copy(
                src_ref=ins[i].at[peer] if each[i] else ins[i],
                dst_ref=outs[i].at[me],
                send_sem=send_sem.at[i, at],
                recv_sem=recv_sem.at[i, at],
                device_id={"tensor": peer},
                device_id_type=pl.DeviceIdType.MESH,
            )
            copy.start()
            copies.append(copy)
    for copy in locals_here + copies:
        copy.wait()


def exchange(ident, each, *arrays):
    count = lax.axis_size("tensor")
    if count != KVH:
        return [
            lax.all_to_all(
                a if e else jnp.broadcast_to(a[None], (count,) + a.shape), "tensor", 0, 0
            )
            for e, a in zip(each, arrays)
        ]
    k = len(arrays)
    shapes = [a.shape if e else (count,) + a.shape for e, a in zip(each, arrays)]
    vmem = pl.BlockSpec(memory_space=pltpu.VMEM)
    return pl.pallas_call(
        functools.partial(exchange_kernel, count, each),
        out_shape=[jax.ShapeDtypeStruct(d, a.dtype) for d, a in zip(shapes, arrays)],
        in_specs=[vmem] * k,
        out_specs=[vmem] * k,
        scratch_shapes=[
            pltpu.SemaphoreType.DMA((k, count - 1)),
            pltpu.SemaphoreType.DMA((k, count - 1)),
            pltpu.SemaphoreType.DMA((k,)),
        ],
        compiler_params=pltpu.CompilerParams(
            collective_id=ident, has_side_effects=True, vmem_limit_bytes=16 * 2**20
        ),
    )(*arrays)


def greet(me, count):
    beside = me + 1 - 2 * lax.rem(me, 2)
    along = [lax.rem(me + 2 * o, count) for o in range(1, count // 2)]
    barrier = pltpu.get_barrier_semaphore()
    for peer in [beside] + along:
        pl.semaphore_signal(
            barrier, inc=1, device_id={"tensor": peer}, device_id_type=pl.DeviceIdType.MESH
        )
    pl.semaphore_wait(barrier, count // 2)
    return beside, along


def push(source, target, sems, at, peer):
    copy = pltpu.make_async_remote_copy(
        src_ref=source,
        dst_ref=target,
        send_sem=sems[0].at[at],
        recv_sem=sems[1].at[at],
        device_id={"tensor": peer},
        device_id_type=pl.DeviceIdType.MESH,
    )
    copy.start()
    return copy


def gather_kernel(count, own, out, send_sem, recv_sem, local_sem):
    me = lax.axis_index("tensor")
    half = count // 2
    sems = (send_sem, recv_sem)
    beside, along = greet(me, count)
    offsets = sorted(range(1, half), key=lambda o: min(o, half - o))
    first = {o: push(own, out.at[me], sems, o, along[o - 1]) for o in offsets}
    rest = [push(own, out.at[me], sems, 0, beside)]
    here = pltpu.make_async_copy(own, out.at[me], local_sem)
    here.start()
    for o in offsets:
        first[o].wait_recv()
        block = out.at[lax.rem(me + count - 2 * o, count)]
        rest.append(push(block, block, sems, half - 1 + o, beside))
    for o in offsets:
        first[o].wait_send()
    for copy in rest:
        copy.wait()
    here.wait()


def gather(ident, array):
    count = lax.axis_size("tensor")
    if count != KVH:
        return exchange(ident, (False,), array)[0]
    vmem = pl.BlockSpec(memory_space=pltpu.VMEM)
    return pl.pallas_call(
        functools.partial(gather_kernel, count),
        out_shape=jax.ShapeDtypeStruct((count,) + array.shape, array.dtype),
        in_specs=[vmem],
        out_specs=vmem,
        scratch_shapes=[
            pltpu.SemaphoreType.DMA((count - 1,)),
            pltpu.SemaphoreType.DMA((count - 1,)),
            pltpu.SemaphoreType.DMA,
        ],
        compiler_params=pltpu.CompilerParams(
            collective_id=ident, has_side_effects=True, vmem_limit_bytes=16 * 2**20
        ),
    )(array)


def sums_kernel(count, sent, out, near, stage, send_sem, recv_sem):
    me = lax.axis_index("tensor")
    half = count // 2
    sems = (send_sem, recv_sem)
    beside, along = greet(me, count)
    mine = me // 2
    targets = along + [me]
    side = lax.rem(me, 2)
    copies = []
    for at, target in enumerate(targets):
        other = target + 1 - 2 * side
        copies.append(push(sent.at[other], near.at[at], sems, at, beside))
    for at, target in enumerate(targets):
        copies[at].wait_recv()
        added = (sent[target].astype(F32) + near[at].astype(F32)).astype(sent.dtype)
        if at < half - 1:
            stage[at] = added
            copies.append(push(stage.at[at], out.at[mine], sems, half + at, target))
        else:
            out[mine] = added
    for copy in copies[:half]:
        copy.wait_send()
    for copy in copies[half:]:
        copy.wait()


def sums(ident, array):
    count = lax.axis_size("tensor")
    if count != KVH:
        return jnp.sum(exchange(ident, (True,), array)[0].astype(F32), 0)
    half = count // 2
    vmem = pl.BlockSpec(memory_space=pltpu.VMEM)
    parts = pl.pallas_call(
        functools.partial(sums_kernel, count),
        out_shape=jax.ShapeDtypeStruct((half,) + array.shape[1:], array.dtype),
        in_specs=[vmem],
        out_specs=vmem,
        scratch_shapes=[
            pltpu.VMEM((half,) + array.shape[1:], array.dtype),
            pltpu.VMEM((half - 1,) + array.shape[1:], array.dtype),
            pltpu.SemaphoreType.DMA((count - 1,)),
            pltpu.SemaphoreType.DMA((count - 1,)),
        ],
        compiler_params=pltpu.CompilerParams(
            collective_id=ident, has_side_effects=True, vmem_limit_bytes=16 * 2**20
        ),
    )(array)
    return jnp.sum(parts.astype(F32), 0)


def pair(value, axis):
    if lax.axis_size("fsdp") != 2:
        return lax.all_gather(value, "fsdp", axis=axis, tiled=True)
    other = lax.ppermute(value, "fsdp", [(0, 1), (1, 0)])
    first = lax.axis_index("fsdp") == 0
    return jnp.concatenate(
        [jnp.where(first, value, other), jnp.where(first, other, value)], axis
    )


def attend(grouped, key_cache, value_cache, live_count):
    rows, cache = key_cache.shape[:2]
    keys = key_cache.reshape(rows, cache, KVH, HD)
    values = value_cache.reshape(rows, cache, KVH, HD)
    scores = jnp.einsum("krmd,rpkd->krmp", grouped, keys, preferred_element_type=F32)
    scores = scores * HD ** (-0.5)
    slot = jnp.arange(cache, dtype=jnp.int32)
    live = (slot[None, :] < live_count[:, None])[None, :, None, :]
    peak = jnp.max(jnp.where(live, scores, F32(-1e30)), -1)
    weights = jnp.where(live, jnp.exp(scores - peak[..., None]), F32(0.0))
    mixed = jnp.einsum("krmp,rpkd->krmd", weights.astype(BF16), values, preferred_element_type=F32)
    return mixed.astype(BF16), peak, jnp.sum(weights, -1)


def shards(
    hidden, lengths, key_cache, value_cache, w_query, w_key, w_value, w_out,
    down_q, up_q, down_o, up_o, out_gain,
):
    tc = lax.axis_size("tensor")
    ti = lax.axis_index("tensor")
    rows = hidden.shape[1]
    width = hidden.shape[2]
    hh = w_query.shape[1] // HD
    scale = HD ** (-0.5)
    share = width // tc
    cache = key_cache.shape[1]
    n = STEPS * rows
    x = hidden.reshape(n, width)
    up_flat = pair(up_q, 2).reshape(R, hh * HD)
    down_flat = pair(down_o, 1).reshape(hh * HD, R)
    nf = lax.axis_size("fsdp")
    chunk = down_q.shape[0]
    spots = [(c, (c % nf) * tc + c // nf) for c in range(nf * tc)]
    up_cols = pair(lax.ppermute(up_o, ("fsdp", "tensor"), spots), 1)
    down_pair = pair(down_q, 0)
    x_pair = jnp.concatenate(
        [
            lax.dynamic_slice_in_dim(x, (f * tc + ti) * chunk, chunk, 1)
            for f in range(nf)
        ],
        1,
    )
    thin = dot(x_pair, down_pair)
    thin = jnp.concatenate([thin, jnp.zeros_like(thin)], 1)
    thin = jnp.sum(exchange(0, (False,), thin)[0], 0)[:, :R]
    position = (lengths[None, :] + jnp.arange(STEPS, dtype=jnp.int32)[:, None]).astype(F32)
    query = dot(x, w_query) + dot(thin.astype(BF16), up_flat)
    query = rotate(query.reshape(STEPS, rows, hh, HD), position[:, :, None]).astype(BF16)
    key_raw = dot(x, w_key).astype(BF16)
    value_new = dot(x, w_value).astype(BF16)
    if hh != GROUP:
        key_raw = lax.all_gather(key_raw, "tensor", axis=1, tiled=True)
        value_new = lax.all_gather(value_new, "tensor", axis=1, tiled=True)
        kv_at = (ti * hh) // GROUP * HD
        key_raw = lax.dynamic_slice_in_dim(key_raw, kv_at, HD, 1)
        value_new = lax.dynamic_slice_in_dim(value_new, kv_at, HD, 1)
    key_raw = key_raw.astype(F32).reshape(STEPS, rows, HD)
    key_new = rotate(key_raw, position).astype(BF16)
    value_new = value_new.reshape(STEPS, rows, HD)

    query, up_cols, down_flat = lax.optimization_barrier((query, up_cols, down_flat))
    query_all = gather(1, query.reshape(n, hh * HD))
    per = tc // KVH
    grouped = query_all.reshape(KVH, per, STEPS, rows, hh, HD).transpose(0, 3, 2, 1, 4, 5)
    grouped = grouped.reshape(KVH, rows, STEPS * GROUP, HD)
    mixed, peak, wsum = attend(grouped, key_cache, value_cache, lengths - ti * cache)
    mixed = mixed.reshape(KVH, rows, STEPS, per, hh, HD).transpose(0, 3, 1, 2, 4, 5)
    mixed = mixed.reshape(tc, n * hh, HD)
    stats = jnp.stack([peak, wsum], 2).reshape(KVH, rows, 2, STEPS, per, hh)
    stats = stats.transpose(0, 4, 1, 2, 3, 5).reshape(tc, n * hh // 64, 128)
    got_mixed, got_stats = exchange(2, (True, True), mixed, stats)
    got_mixed = got_mixed.astype(F32).reshape(tc, rows, STEPS, hh, HD)
    got_stats = got_stats.reshape(tc, rows, 2, STEPS, hh)
    got_peak = got_stats[:, :, 0]
    got_sum = got_stats[:, :, 1]

    own = (
        jnp.einsum("srhd,trd->rsht", query, key_new, preferred_element_type=F32) * scale
    )
    causal = jnp.tril(jnp.ones((STEPS, STEPS), bool))[None, :, None, :]
    own_peak = jnp.max(jnp.where(causal, own, F32(-1e30)), -1)
    top = jnp.maximum(jnp.max(got_peak, 0), own_peak)
    own_w = jnp.where(causal, jnp.exp(own - top[..., None]), F32(0.0))
    far = jnp.exp(got_peak - top[None])
    den = jnp.sum(far * got_sum, 0) + jnp.sum(own_w, -1)
    num = jnp.sum(far[..., None] * got_mixed, 0) + jnp.einsum(
        "rsht,trd->rshd", own_w.astype(BF16), value_new, preferred_element_type=F32
    )
    attended = (num / den[..., None]).astype(BF16).transpose(1, 0, 2, 3).reshape(n, hh * HD)
    part = dot(attended, w_out).astype(BF16).reshape(n, tc, share).transpose(1, 0, 2)
    thin_out = dot(attended, down_flat)
    high = thin_out.astype(BF16)
    low = (thin_out - high.astype(F32)).astype(BF16)
    both = jnp.broadcast_to(jnp.concatenate([high, low], 1)[None], (tc, n, 2 * R))
    sent = jnp.concatenate([part, both], 2)
    total = sums(3, sent)
    thin_out = (total[:, share : share + R] + total[:, share + R :]).astype(BF16)
    own_cols = total[:, :share] + dot(thin_out, up_cols)
    own_cols = own_cols + lax.dynamic_slice_in_dim(x, ti * share, share, 1).astype(F32)
    square = jnp.sum(own_cols * own_cols, -1, keepdims=True)
    square = jnp.sum(exchange(4, (False,), jnp.broadcast_to(square, (n, 128)))[0], 0)
    factor = lax.rsqrt(square[:, :1] / width + norm_eps)
    return (own_cols * factor * out_gain.astype(F32)).astype(BF16).reshape(STEPS, rows, share)


def solution(mesh):
    both = ("groups", "fsdp")
    placed = (
        P(None, both, None),
        P(both),
        P(both, "tensor", None),
        P(both, "tensor", None),
        P(None, "tensor"),
        P(None, "tensor"),
        P(None, "tensor"),
        P("tensor", None),
        P(("groups", "fsdp", "tensor"), None),
        P(None, ("groups", "tensor"), "fsdp"),
        P("tensor", both, None),
        P(None, ("groups", "fsdp", "tensor")),
        P("tensor"),
    )
    return jax.shard_map(
        shards,
        mesh=mesh,
        in_specs=placed,
        out_specs=P(None, both, "tensor"),
        check_vma=False,
    )
```

```python
import functools
import math

import jax
import jax.numpy as jnp
from jax import lax
from jax.experimental import pallas as pl
from jax.experimental.pallas import tpu as pltpu
from jax.sharding import PartitionSpec as P

HEADS = 64
KVH = 8
HD = 128
R = 64
STEPS = 4
GROUP = HEADS // KVH

rope_base = 1000000.0
norm_eps = 1e-06
F32 = jnp.float32
BF16 = jnp.bfloat16


def rotate(values_in, position):
    half_dim = values_in.shape[-1] // 2
    exponent = jnp.arange(half_dim, dtype=F32) * (2.0 / values_in.shape[-1])
    frequency = jnp.exp(-exponent * math.log(rope_base))
    angles = position[..., None] * frequency
    cosine = jnp.cos(angles)
    sine = jnp.sin(angles)
    first_half = values_in[..., :half_dim]
    second_half = values_in[..., half_dim:]
    return jnp.concatenate(
        [first_half * cosine - second_half * sine, second_half * cosine + first_half * sine], -1
    )


def dot(a, b):
    return jnp.dot(a, b, preferred_element_type=F32)


def exchange_kernel(count, each, *refs):
    k = len(each)
    ins, outs = refs[:k], refs[k : 2 * k]
    send_sem, recv_sem, local_sem = refs[2 * k :]
    me = lax.axis_index("tensor")
    barrier = pltpu.get_barrier_semaphore()
    peers = [lax.rem(me + offset, count) for offset in range(1, count)]
    for peer in peers:
        pl.semaphore_signal(
            barrier, inc=1, device_id={"tensor": peer}, device_id_type=pl.DeviceIdType.MESH
        )
    locals_here = []
    for i in range(k):
        source = ins[i].at[me] if each[i] else ins[i]
        locals_here.append(pltpu.make_async_copy(source, outs[i].at[me], local_sem.at[i]))
        locals_here[-1].start()
    pl.semaphore_wait(barrier, count - 1)
    copies = []
    for at, peer in enumerate(peers):
        for i in range(k):
            copy = pltpu.make_async_remote_copy(
                src_ref=ins[i].at[peer] if each[i] else ins[i],
                dst_ref=outs[i].at[me],
                send_sem=send_sem.at[i, at],
                recv_sem=recv_sem.at[i, at],
                device_id={"tensor": peer},
                device_id_type=pl.DeviceIdType.MESH,
            )
            copy.start()
            copies.append(copy)
    for copy in locals_here + copies:
        copy.wait()


def exchange(ident, each, *arrays):
    count = lax.axis_size("tensor")
    if count != KVH:
        return [
            lax.all_to_all(
                a if e else jnp.broadcast_to(a[None], (count,) + a.shape), "tensor", 0, 0
            )
            for e, a in zip(each, arrays)
        ]
    k = len(arrays)
    shapes = [a.shape if e else (count,) + a.shape for e, a in zip(each, arrays)]
    vmem = pl.BlockSpec(memory_space=pltpu.VMEM)
    return pl.pallas_call(
        functools.partial(exchange_kernel, count, each),
        out_shape=[jax.ShapeDtypeStruct(d, a.dtype) for d, a in zip(shapes, arrays)],
        in_specs=[vmem] * k,
        out_specs=[vmem] * k,
        scratch_shapes=[
            pltpu.SemaphoreType.DMA((k, count - 1)),
            pltpu.SemaphoreType.DMA((k, count - 1)),
            pltpu.SemaphoreType.DMA((k,)),
        ],
        compiler_params=pltpu.CompilerParams(
            collective_id=ident, has_side_effects=True, vmem_limit_bytes=16 * 2**20
        ),
    )(*arrays)


def greet(me, count):
    beside = me + 1 - 2 * lax.rem(me, 2)
    along = [lax.rem(me + 2 * o, count) for o in range(1, count // 2)]
    barrier = pltpu.get_barrier_semaphore()
    for peer in [beside] + along:
        pl.semaphore_signal(
            barrier, inc=1, device_id={"tensor": peer}, device_id_type=pl.DeviceIdType.MESH
        )
    pl.semaphore_wait(barrier, count // 2)
    return beside, along


def push(source, target, sems, at, peer):
    copy = pltpu.make_async_remote_copy(
        src_ref=source,
        dst_ref=target,
        send_sem=sems[0].at[at],
        recv_sem=sems[1].at[at],
        device_id={"tensor": peer},
        device_id_type=pl.DeviceIdType.MESH,
    )
    copy.start()
    return copy


def gather_kernel(count, own, out, send_sem, recv_sem, local_sem):
    me = lax.axis_index("tensor")
    half = count // 2
    sems = (send_sem, recv_sem)
    beside, along = greet(me, count)
    offsets = sorted(range(1, half), key=lambda o: min(o, half - o))
    first = {o: push(own, out.at[me], sems, o, along[o - 1]) for o in offsets}
    rest = [push(own, out.at[me], sems, 0, beside)]
    here = pltpu.make_async_copy(own, out.at[me], local_sem)
    here.start()
    for o in offsets:
        first[o].wait_recv()
        block = out.at[lax.rem(me + count - 2 * o, count)]
        rest.append(push(block, block, sems, half - 1 + o, beside))
    for o in offsets:
        first[o].wait_send()
    for copy in rest:
        copy.wait()
    here.wait()


def gather(ident, array):
    count = lax.axis_size("tensor")
    if count != KVH:
        return exchange(ident, (False,), array)[0]
    vmem = pl.BlockSpec(memory_space=pltpu.VMEM)
    return pl.pallas_call(
        functools.partial(gather_kernel, count),
        out_shape=jax.ShapeDtypeStruct((count,) + array.shape, array.dtype),
        in_specs=[vmem],
        out_specs=vmem,
        scratch_shapes=[
            pltpu.SemaphoreType.DMA((count - 1,)),
            pltpu.SemaphoreType.DMA((count - 1,)),
            pltpu.SemaphoreType.DMA,
        ],
        compiler_params=pltpu.CompilerParams(
            collective_id=ident, has_side_effects=True, vmem_limit_bytes=16 * 2**20
        ),
    )(array)


def sums_kernel(count, sent, out, near, stage, send_sem, recv_sem):
    me = lax.axis_index("tensor")
    half = count // 2
    sems = (send_sem, recv_sem)
    beside, along = greet(me, count)
    mine = me // 2
    targets = along + [me]
    side = lax.rem(me, 2)
    copies = []
    for at, target in enumerate(targets):
        other = target + 1 - 2 * side
        copies.append(push(sent.at[other], near.at[at], sems, at, beside))
    for at, target in enumerate(targets):
        copies[at].wait_recv()
        added = (sent[target].astype(F32) + near[at].astype(F32)).astype(sent.dtype)
        if at < half - 1:
            stage[at] = added
            copies.append(push(stage.at[at], out.at[mine], sems, half + at, target))
        else:
            out[mine] = added
    for copy in copies[:half]:
        copy.wait_send()
    for copy in copies[half:]:
        copy.wait()


def sums(ident, array):
    count = lax.axis_size("tensor")
    if count != KVH:
        return jnp.sum(exchange(ident, (True,), array)[0].astype(F32), 0)
    half = count // 2
    vmem = pl.BlockSpec(memory_space=pltpu.VMEM)
    parts = pl.pallas_call(
        functools.partial(sums_kernel, count),
        out_shape=jax.ShapeDtypeStruct((half,) + array.shape[1:], array.dtype),
        in_specs=[vmem],
        out_specs=vmem,
        scratch_shapes=[
            pltpu.VMEM((half,) + array.shape[1:], array.dtype),
            pltpu.VMEM((half - 1,) + array.shape[1:], array.dtype),
            pltpu.SemaphoreType.DMA((count - 1,)),
            pltpu.SemaphoreType.DMA((count - 1,)),
        ],
        compiler_params=pltpu.CompilerParams(
            collective_id=ident, has_side_effects=True, vmem_limit_bytes=16 * 2**20
        ),
    )(array)
    return jnp.sum(parts.astype(F32), 0)


CUTS = 4


def thin_kernel(count, own, x, weight, out, based, held, send_sem, recv_sem, local_sem, load_sem):
    me = lax.axis_index("tensor")
    depth = weight.shape[0] // CUTS
    loads = []
    for c in range(CUTS):
        source = weight.at[pl.ds(c * depth, depth)]
        loads.append(pltpu.make_async_copy(source, held.at[c], load_sem.at[c]))
        loads[-1].start()
    barrier = pltpu.get_barrier_semaphore()
    peers = [lax.rem(me + offset, count) for offset in range(1, count)]
    for peer in peers:
        pl.semaphore_signal(
            barrier, inc=1, device_id={"tensor": peer}, device_id_type=pl.DeviceIdType.MESH
        )
    here = pltpu.make_async_copy(own, out.at[me], local_sem)
    here.start()
    pl.semaphore_wait(barrier, count - 1)
    sems = (send_sem, recv_sem)
    copies = [push(own, out.at[me], sems, at, peer) for at, peer in enumerate(peers)]
    for c in range(CUTS):
        loads[c].wait()
        part = dot(x[:, c * depth : (c + 1) * depth], held[c])
        based[...] = part if c == 0 else based[...] + part
    for copy in copies:
        copy.wait()
    here.wait()


def exchange_and_dot(ident, own, x, weight):
    count = lax.axis_size("tensor")
    if count != KVH:
        return exchange(ident, (False,), own)[0], dot(x, weight)
    vmem = pl.BlockSpec(memory_space=pltpu.VMEM)
    depth, cols = weight.shape
    return pl.pallas_call(
        functools.partial(thin_kernel, count),
        out_shape=[
            jax.ShapeDtypeStruct((count,) + own.shape, own.dtype),
            jax.ShapeDtypeStruct((x.shape[0], cols), F32),
        ],
        in_specs=[vmem, vmem, pl.BlockSpec(memory_space=pl.ANY)],
        out_specs=[vmem, vmem],
        scratch_shapes=[
            pltpu.VMEM((CUTS, depth // CUTS, cols), weight.dtype),
            pltpu.SemaphoreType.DMA((count - 1,)),
            pltpu.SemaphoreType.DMA((count - 1,)),
            pltpu.SemaphoreType.DMA,
            pltpu.SemaphoreType.DMA((CUTS,)),
        ],
        compiler_params=pltpu.CompilerParams(
            collective_id=ident, has_side_effects=True, vmem_limit_bytes=32 * 2**20
        ),
    )(own, x, weight)


def pair(value, axis):
    if lax.axis_size("fsdp") != 2:
        return lax.all_gather(value, "fsdp", axis=axis, tiled=True)
    other = lax.ppermute(value, "fsdp", [(0, 1), (1, 0)])
    first = lax.axis_index("fsdp") == 0
    return jnp.concatenate(
        [jnp.where(first, value, other), jnp.where(first, other, value)], axis
    )


def attend(grouped, key_cache, value_cache, live_count):
    rows, cache = key_cache.shape[:2]
    keys = key_cache.reshape(rows, cache, KVH, HD)
    values = value_cache.reshape(rows, cache, KVH, HD)
    scores = jnp.einsum("krmd,rpkd->krmp", grouped, keys, preferred_element_type=F32)
    scores = scores * HD ** (-0.5)
    slot = jnp.arange(cache, dtype=jnp.int32)
    live = (slot[None, :] < live_count[:, None])[None, :, None, :]
    peak = jnp.max(jnp.where(live, scores, F32(-1e30)), -1)
    weights = jnp.where(live, jnp.exp(scores - peak[..., None]), F32(0.0))
    mixed = jnp.einsum("krmp,rpkd->krmd", weights.astype(BF16), values, preferred_element_type=F32)
    return mixed.astype(BF16), peak, jnp.sum(weights, -1)


def shards(
    hidden, lengths, key_cache, value_cache, w_query, w_key, w_value, w_out,
    down_q, up_q, down_o, up_o, out_gain,
):
    tc = lax.axis_size("tensor")
    ti = lax.axis_index("tensor")
    rows = hidden.shape[1]
    width = hidden.shape[2]
    hh = w_query.shape[1] // HD
    scale = HD ** (-0.5)
    share = width // tc
    cache = key_cache.shape[1]
    n = STEPS * rows
    x = hidden.reshape(n, width)
    up_flat = pair(up_q, 2).reshape(R, hh * HD)
    down_flat = pair(down_o, 1).reshape(hh * HD, R)
    nf = lax.axis_size("fsdp")
    chunk = down_q.shape[0]
    spots = [(c, (c % nf) * tc + c // nf) for c in range(nf * tc)]
    up_cols = pair(lax.ppermute(up_o, ("fsdp", "tensor"), spots), 1)
    down_pair = pair(down_q, 0)
    x_pair = jnp.concatenate(
        [
            lax.dynamic_slice_in_dim(x, (f * tc + ti) * chunk, chunk, 1)
            for f in range(nf)
        ],
        1,
    )
    thin = dot(x_pair, down_pair)
    thin = jnp.concatenate([thin[: n // 2], thin[n // 2 :]], 1)
    thin, based = exchange_and_dot(0, thin, x, w_query)
    thin = jnp.sum(thin, 0)
    thin = jnp.concatenate([thin[:, :R], thin[:, R:]], 0)
    position = (lengths[None, :] + jnp.arange(STEPS, dtype=jnp.int32)[:, None]).astype(F32)
    query = based + dot(thin.astype(BF16), up_flat)
    query = rotate(query.reshape(STEPS, rows, hh, HD), position[:, :, None]).astype(BF16)
    key_raw = dot(x, w_key).astype(BF16)
    value_new = dot(x, w_value).astype(BF16)
    if hh != GROUP:
        key_raw = lax.all_gather(key_raw, "tensor", axis=1, tiled=True)
        value_new = lax.all_gather(value_new, "tensor", axis=1, tiled=True)
        kv_at = (ti * hh) // GROUP * HD
        key_raw = lax.dynamic_slice_in_dim(key_raw, kv_at, HD, 1)
        value_new = lax.dynamic_slice_in_dim(value_new, kv_at, HD, 1)
    key_raw = key_raw.astype(F32).reshape(STEPS, rows, HD)
    key_new = rotate(key_raw, position).astype(BF16)
    value_new = value_new.reshape(STEPS, rows, HD)

    query, up_cols, down_flat = lax.optimization_barrier((query, up_cols, down_flat))
    query_all = gather(1, query.reshape(n, hh * HD))
    per = tc // KVH
    grouped = query_all.reshape(KVH, per, STEPS, rows, hh, HD).transpose(0, 3, 2, 1, 4, 5)
    grouped = grouped.reshape(KVH, rows, STEPS * GROUP, HD)
    mixed, peak, wsum = attend(grouped, key_cache, value_cache, lengths - ti * cache)
    mixed = mixed.reshape(KVH, rows, STEPS, per, hh, HD).transpose(0, 3, 1, 2, 4, 5)
    mixed = mixed.reshape(tc, n * hh, HD)
    stats = jnp.stack([peak, wsum], 2).reshape(KVH, rows, 2, STEPS, per, hh)
    stats = stats.transpose(0, 4, 1, 2, 3, 5).reshape(tc, n * hh // 64, 128)
    got_mixed, got_stats = exchange(2, (True, True), mixed, stats)
    got_mixed = got_mixed.astype(F32).reshape(tc, rows, STEPS, hh, HD)
    got_stats = got_stats.reshape(tc, rows, 2, STEPS, hh)
    got_peak = got_stats[:, :, 0]
    got_sum = got_stats[:, :, 1]

    own = (
        jnp.einsum("srhd,trd->rsht", query, key_new, preferred_element_type=F32) * scale
    )
    causal = jnp.tril(jnp.ones((STEPS, STEPS), bool))[None, :, None, :]
    own_peak = jnp.max(jnp.where(causal, own, F32(-1e30)), -1)
    top = jnp.maximum(jnp.max(got_peak, 0), own_peak)
    own_w = jnp.where(causal, jnp.exp(own - top[..., None]), F32(0.0))
    far = jnp.exp(got_peak - top[None])
    den = jnp.sum(far * got_sum, 0) + jnp.sum(own_w, -1)
    num = jnp.sum(far[..., None] * got_mixed, 0) + jnp.einsum(
        "rsht,trd->rshd", own_w.astype(BF16), value_new, preferred_element_type=F32
    )
    attended = (num / den[..., None]).astype(BF16).transpose(1, 0, 2, 3).reshape(n, hh * HD)
    part = dot(attended, w_out).astype(BF16).reshape(n, tc, share).transpose(1, 0, 2)
    thin_out = dot(attended, down_flat)
    high = thin_out.astype(BF16)
    low = (thin_out - high.astype(F32)).astype(BF16)
    both = jnp.broadcast_to(jnp.concatenate([high, low], 1)[None], (tc, n, 2 * R))
    sent = jnp.concatenate([part, both], 2)
    total = sums(3, sent)
    thin_out = (total[:, share : share + R] + total[:, share + R :]).astype(BF16)
    own_cols = total[:, :share] + dot(thin_out, up_cols)
    own_cols = own_cols + lax.dynamic_slice_in_dim(x, ti * share, share, 1).astype(F32)
    square = jnp.pad(jnp.sum(own_cols * own_cols, -1), (0, -n % 128))
    square = jnp.broadcast_to(square[None], (8, square.shape[0]))
    square = jnp.sum(exchange(4, (False,), square)[0][:, 0], 0)[:n, None]
    factor = lax.rsqrt(square / width + norm_eps)
    return (own_cols * factor * out_gain.astype(F32)).astype(BF16).reshape(STEPS, rows, share)


def solution(mesh):
    both = ("groups", "fsdp")
    placed = (
        P(None, both, None),
        P(both),
        P(both, "tensor", None),
        P(both, "tensor", None),
        P(None, "tensor"),
        P(None, "tensor"),
        P(None, "tensor"),
        P("tensor", None),
        P(("groups", "fsdp", "tensor"), None),
        P(None, ("groups", "tensor"), "fsdp"),
        P("tensor", both, None),
        P(None, ("groups", "fsdp", "tensor")),
        P("tensor"),
    )
    return jax.shard_map(
        shards,
        mesh=mesh,
        in_specs=placed,
        out_specs=P(None, both, "tensor"),
        check_vma=False,
    )
```
